256 devices in a mesh: section: 32 (over y, z_lo, core), head: 8 (over x, z_hi).
Axes of the slice: x: 4, y: 4, z: 8 (z_hi: 2, z_lo: 4; z = z_hi * 4 + z_lo), core: 2. Of those that a mesh axis runs over, the one named last changes fastest.
Arguments:
- carry_x: bfloat16 [32, 384, 1152], P('section', 'head'), may hold values from -6 to 6
- kv_buffer: bfloat16 [32, 2, 1152, 6144], P('section', None, 'head'), may hold values from -48 to 48, as said below
- qkv_weight: bfloat16 [32, 3, 1152, 1152], P('section', None, 'head'), may hold values from -0.1875 to 0.1875
- out_weight: bfloat16 [32, 1152, 1152], P('section', 'head'), may hold values from -0.1875 to 0.1875
- up_weight: bfloat16 [32, 1152, 4608], P('section', None, 'head'), may hold values from -0.1875 to 0.1875
- down_weight: bfloat16 [32, 1152, 4608], P('section', None, 'head'), may hold values from -0.09375 to 0.09375
- time_table: float32 [20, 6, 1152], replicated, may hold values from -3 to 3
- block_table: float32 [32, 6, 1152], P('section'), may hold values from -3 to 3
- time_index: int32 [32], P('section'), may hold values from 0 to 19
- patch_order: int32 [16], replicated, may hold values from 0 to 15, each once
Outputs:
- next_x: bfloat16 [32, 384, 1152], P('section', 'head')
- fresh_kv: bfloat16 [32, 2, 2, 1152, 384], P('section', None, None, 'head')
The draws below stay inside these ranges and needn't reach their ends.
Inputs may be any that keep to these rules, and one draw needn't show every extreme that they name: `kv_buffer`: cached keys and values.
All inputs are finite; a program needn't handle non-finite values.
Results may differ from the reference program's by a relative error of at most 0.034.
Values may be sent and summed in bfloat16 or wider, within the bound.
No kernel may reach another device: no remote copies, remote signals or barrier semaphores. Data moves between devices by JAX's collectives and lax.ppermute only.
A program may use at most 128 MiB of HBM per device.

```python
import math
import jax
import jax.numpy as jnp
from jax import lax

D = 1152
HEADS = 16
HEAD_DIM = 72
FF = 4608
PATCH_TOK = 384
PATCHES = 16
MICRO = 2
STEPS = 20
TOKENS = 6144
N_SECTION = 32


def draw_kv_buffer(key, part):
    key = jax.random.fold_in(key, 11)
    shape = (N_SECTION, 2, D, TOKENS)
    base = jnp.clip(jax.random.normal(key, shape, jnp.float32), -6.0, 6.0)
    offset_key = jax.random.fold_in(key, 5)
    offsets = 1.5 * jnp.clip(jax.random.normal(offset_key, (N_SECTION, 2, D, PATCHES), jnp.float32), -4.0, 4.0)
    base = base + jnp.repeat(offsets, PATCH_TOK, axis=3)
    return jnp.clip(base, -48.0, 48.0).astype(jnp.bfloat16)


def set_ends(values, stream_key, least, high):
    longest = values.shape.index(max(values.shape))
    spots = []
    for shift in (0, 1):
        where = [jax.random.randint(jax.random.fold_in(stream_key, axis), (), 0, length) for axis, length in enumerate(values.shape)]
        where[longest] = (where[longest] + shift) % values.shape[longest]
        spots.append(tuple(where))
    return values.at[spots[0]].set(least).at[spots[1]].set(high)


def block_levels(key, extent, cuts, least, high):
    loudness, own = 1.0, jax.random.fold_in(key, 6)
    for dim, shards_of in cuts:
        steps = jnp.exp(jax.random.uniform(jax.random.fold_in(own, dim), (shards_of,), jnp.float32, least / len(cuts), high / len(cuts)))
        loudness = loudness * jnp.repeat(steps, extent[dim] // shards_of).reshape([-1 if axis == dim else 1 for axis in range(len(extent))])
    return loudness


def centred(own_key, extent, scale, most, shards=(), kind=jnp.bfloat16):
    drawn = jax.random.normal(own_key, extent, jnp.float32) * scale
    if len(shards) > 0:
        drawn = block_levels(own_key, extent, shards, -0.22, 0.18) * drawn
    return jnp.clip(drawn, min=-most, max=most).astype(kind)


def setup_inputs(seed: int = 0) -> dict:
    keys = jax.random.split(jax.random.key(seed), 11)
    return {
        "carry_x": centred(keys[0], (N_SECTION, PATCH_TOK, D), 1.0, 6.0, ((0, 32), (1, 8))),
        "kv_buffer": draw_kv_buffer(jax.random.fold_in(keys[10], 71), 0),
        "qkv_weight": centred(keys[2], (N_SECTION, 3, D, D), D ** -0.5, 0.1875, ((0, 32), (2, 8))),
        "out_weight": centred(keys[3], (N_SECTION, D, D), D ** -0.5, 0.1875, ((0, 32), (1, 8))),
        "up_weight": centred(keys[4], (N_SECTION, D, FF), D ** -0.5, 0.1875, ((0, 32), (2, 8))),
        "down_weight": centred(keys[5], (N_SECTION, D, FF), FF ** -0.5, 0.09375, ((0, 32), (2, 8))),
        "time_table": centred(keys[6], (STEPS, 6, D), 0.5, 3.0, (), jnp.float32),
        "block_table": centred(keys[7], (N_SECTION, 6, D), 0.5, 3.0, ((0, 32),), jnp.float32),
        "time_index": set_ends(jax.random.randint(keys[8], (N_SECTION,), 0, STEPS), jax.random.fold_in(keys[8], 1), 0, STEPS - 1).astype(jnp.int32),
        "patch_order": jax.random.permutation(keys[9], PATCHES).astype(jnp.int32),
    }


def layer_norm(values_in):
    center = values_in - lax.optimization_barrier(jnp.mean(values_in, axis=-1, keepdims=True))
    spread = lax.optimization_barrier(jnp.mean(center * center, axis=-1, keepdims=True))
    return center * lax.rsqrt(spread + 1e-06)

def patch_of(patch_order, section_index, micro):
    position = (micro - section_index) % PATCHES
    picked = jnp.where(jnp.arange(PATCHES) == position, patch_order, 0)
    return jnp.sum(picked).astype(jnp.int32)

def attend(queries, key_cache, value_cache):
    head_queries = queries.astype(jnp.float32).reshape(queries.shape[0], HEADS, HEAD_DIM)
    head_keys = key_cache.astype(jnp.float32).reshape(HEADS, HEAD_DIM, key_cache.shape[1])
    head_values = value_cache.astype(jnp.float32).reshape(HEADS, HEAD_DIM, value_cache.shape[1])
    scores = jnp.einsum('qhd,hdk->hqk', head_queries, head_keys) / math.sqrt(HEAD_DIM)
    probs = jax.nn.softmax(scores, axis=-1).astype(jnp.bfloat16)
    attended = jnp.einsum('hqk,hdk->qhd', probs.astype(jnp.float32), head_values)
    return attended.astype(jnp.bfloat16).reshape(queries.shape[0], D)

def one_section(inputs, buffer_pair, w_qkv, w_out, w_up, w_down, modulation, patch):
    inputs_f = inputs.astype(jnp.float32)
    attn_in = (layer_norm(inputs_f) * (1.0 + modulation[1]) + modulation[0]).astype(jnp.bfloat16)
    projected = lax.dot_general(attn_in, w_qkv.reshape(3 * D, D), (((1,), (1,)), ((), ())), preferred_element_type=jnp.float32)
    projected = projected.astype(jnp.bfloat16).reshape(PATCH_TOK, 3, D)
    queries, new_keys, new_values = (projected[:, 0], projected[:, 1], projected[:, 2])
    first_row = (patch * PATCH_TOK).astype(jnp.int32)
    key_cache = lax.dynamic_update_slice(buffer_pair[0], new_keys.T, (jnp.int32(0), first_row))
    value_cache = lax.dynamic_update_slice(buffer_pair[1], new_values.T, (jnp.int32(0), first_row))
    attended = attend(queries, key_cache, value_cache)
    mixed = jnp.dot(attended, w_out, preferred_element_type=jnp.float32)
    after_attn = inputs_f + modulation[2] * mixed
    mlp_in = (layer_norm(after_attn) * (1.0 + modulation[4]) + modulation[3]).astype(jnp.bfloat16)
    hidden = jax.nn.gelu(jnp.dot(mlp_in, w_up, preferred_element_type=jnp.float32), approximate=True).astype(jnp.bfloat16)
    feedforward = lax.dot_general(hidden, w_down, (((1,), (1,)), ((), ())), preferred_element_type=jnp.float32)
    result = (after_attn + modulation[5] * feedforward).astype(jnp.bfloat16)
    return (result, jnp.stack([new_keys.T, new_values.T]), jnp.stack([key_cache, value_cache]))

def reference(carry_x, kv_buffer, qkv_weight, out_weight, up_weight, down_weight, time_table, block_table, time_index, patch_order):
    chosen = time_index[:, None] == jnp.arange(STEPS)[None, :]
    modulations = lax.optimization_barrier(jnp.sum(jnp.where(chosen[:, :, None, None], time_table[None], jnp.float32(0.0)), axis=1)) + block_table
    activations = carry_x
    buffers = kv_buffer
    fresh_list = []
    for micro in range(MICRO):

        def per_section(packed):
            section_index, inputs, buffer_pair, w_qkv, w_out, w_up, w_down, modulation = packed
            patch = patch_of(patch_order, section_index, micro)
            return one_section(inputs, buffer_pair, w_qkv, w_out, w_up, w_down, modulation, patch)
        outputs, fresh, buffers = lax.map(per_section, (jnp.arange(N_SECTION, dtype=jnp.int32), activations, buffers, qkv_weight, out_weight, up_weight, down_weight, modulations))
        fresh_list.append(fresh)
        activations = jnp.roll(outputs, 1, axis=0)
    return (activations, jnp.stack(fresh_list, axis=1))
```

```python
import functools
import math

import jax
import jax.numpy as jnp
from jax import lax
from jax.experimental import pallas as pl
from jax.experimental.pallas import tpu as pltpu
from jax.sharding import PartitionSpec as P

HEAD_DIM = 72
PATCHES = 16
PATCH_TOK = 384
MICRO = 2
STEPS = 20
COLUMNS = 4
SECTIONS = 32
PAIR = PATCH_TOK // COLUMNS
HALF = PAIR // 2
LOG2_SCALE = math.log2(math.e) / math.sqrt(HEAD_DIM)
NT = (((1,), (1,)), ((), ()))
F32 = jnp.float32
BF16 = jnp.bfloat16
VMEM = pl.BlockSpec(memory_space=pltpu.VMEM)
SMEM = pl.BlockSpec(memory_space=pltpu.SMEM)
ANY = pl.BlockSpec(memory_space=pl.ANY)


def head_of(column, row):
    return (column % COLUMNS) * 2 + row % 2


def flat(section, head):
    return (section % SECTIONS) * 8 + head


ROW_SWAP = [(head_of(c, r), head_of(c, r + 1)) for c in range(COLUMNS) for r in range(2)]


def column_step(step):
    return [(head_of(c, r), head_of(c + step, r)) for c in range(COLUMNS) for r in range(2)]


def section_step(step):
    return [
        (flat(s, head_of(c, r)), flat(s + 1, head_of(c + step, r + (s % 8 == 7))))
        for s in range(SECTIONS)
        for c in range(COLUMNS)
        for r in range(2)
    ]


def swap_rows(value):
    return lax.ppermute(value, "head", ROW_SWAP)


def to_column(value, step):
    return lax.ppermute(value, "head", column_step(step))


def to_section(value, step):
    return lax.ppermute(value, ("section", "head"), section_step(step))


def layer_norm(values_in):
    center = values_in - jnp.mean(values_in, axis=-1, keepdims=True)
    spread = jnp.mean(center * center, axis=-1, keepdims=True)
    return center * lax.rsqrt(spread + 1e-06)


def patch_of(patch_order, section_index, micro):
    position = (micro - section_index) % PATCHES
    picked = jnp.where(jnp.arange(PATCHES) == position, patch_order, 0)
    return jnp.sum(picked)


def attention_kernel(micro, patch_ref, x0, x1, x2, x3, mod, w_qkv, w_out, cache, *rest):
    if micro:
        earlier, rest = rest[0], rest[1:]
    fresh, part0, part1, part2, part3, keys, values, attn_in, queries, scores, sem = rest
    width = w_qkv.shape[1]
    copies = [
        pltpu.make_async_copy(
            cache.at[0, :, pl.ds(c * PATCH_TOK, PATCH_TOK)], keys.at[c], sem.at[0]
        )
        for c in range(PATCHES)
    ] + [
        pltpu.make_async_copy(
            cache.at[1, :, pl.ds(c * PATCH_TOK, PATCH_TOK)],
            values.at[c, pl.ds(0, width)],
            sem.at[1],
        )
        for c in range(PATCHES)
    ]
    for copy in copies:
        copy.start()
    for k, block in enumerate((x0, x1, x2, x3)):
        attn_in[k * PAIR : (k + 1) * PAIR, :] = (
            layer_norm(block[...].astype(F32)) * (1.0 + mod[1:2, :]) + mod[0:1, :]
        ).astype(BF16)
    normed = attn_in[...]
    projected = lax.dot_general(normed, w_qkv[0], NT, preferred_element_type=F32)
    first_head = lax.broadcasted_iota(jnp.int32, (PATCH_TOK, width), 1) < HEAD_DIM
    queries[0:PATCH_TOK, :] = jnp.where(first_head, projected, 0.0).astype(BF16)
    queries[PATCH_TOK : 2 * PATCH_TOK, :] = jnp.where(first_head, 0.0, projected).astype(BF16)
    new_keys = lax.dot_general(w_qkv[1], normed, NT, preferred_element_type=F32).astype(BF16)
    new_values = lax.dot_general(w_qkv[2], normed, NT, preferred_element_type=F32).astype(BF16)
    fresh[0] = new_keys
    fresh[1] = new_values
    values[:, width : width + 16, :] = jnp.ones((PATCHES, 16, PATCH_TOK), BF16)
    for copy in copies:
        copy.wait()
    if micro:
        keys[patch_ref[0]] = earlier[0]
        values[patch_ref[0], 0:width] = earlier[1]
    keys[patch_ref[micro]] = new_keys
    values[patch_ref[micro], 0:width] = new_values
    highest = None
    for c in range(PATCHES):
        block = jnp.dot(queries[...], keys[c], preferred_element_type=F32)
        scores[c] = block
        top = jnp.maximum(jnp.maximum(block[:, 0:128], block[:, 128:256]), block[:, 256:384])
        highest = top if highest is None else jnp.maximum(highest, top)
    offset = jnp.max(highest, axis=1, keepdims=True) * LOG2_SCALE
    total = None
    for c in range(PATCHES):
        probs = jnp.exp2(scores[c] * LOG2_SCALE - offset).astype(BF16)
        product = lax.dot_general(probs, values[c], NT, preferred_element_type=F32)
        total = product if total is None else total + product
    total = total[:, 0:width] / total[:, width : width + 1]
    attended = jnp.where(first_head, total[0:PATCH_TOK], total[PATCH_TOK : 2 * PATCH_TOK])
    mixed = jnp.dot(attended.astype(BF16), w_out[...], preferred_element_type=F32)
    for k, part in enumerate((part0, part1, part2, part3)):
        part[...] = mixed[k * PAIR : (k + 1) * PAIR].astype(BF16)


def attention(micro, patches, blocks, modulation, w_qkv, w_out, cache, earlier):
    width, model = w_qkv.shape[1], w_qkv.shape[2]
    extra = [earlier] if micro else []
    return pl.pallas_call(
        functools.partial(attention_kernel, micro),
        out_shape=[jax.ShapeDtypeStruct((2, width, PATCH_TOK), BF16)]
        + [jax.ShapeDtypeStruct((PAIR, model), BF16)] * COLUMNS,
        in_specs=[SMEM] + [VMEM] * 7 + [ANY] + [VMEM] * len(extra),
        out_specs=[VMEM] * 5,
        scratch_shapes=[
            pltpu.VMEM((PATCHES, width, PATCH_TOK), BF16),
            pltpu.VMEM((PATCHES, width + 16, PATCH_TOK), BF16),
            pltpu.VMEM((PATCH_TOK, model), BF16),
            pltpu.VMEM((2 * PATCH_TOK, width), BF16),
            pltpu.VMEM((PATCHES, 2 * PATCH_TOK, PATCH_TOK), F32),
            pltpu.SemaphoreType.DMA((2,)),
        ],
        compiler_params=pltpu.CompilerParams(vmem_limit_bytes=52 * 2**20),
        cost_estimate=pl.CostEstimate(
            flops=4 * 10**9, bytes_accessed=8 * 10**6, transcendentals=5 * 10**6
        ),
        name="attention",
    )(patches, *blocks, modulation, w_qkv, w_out, cache, *extra)


def mlp_in_kernel(x_ref, own, other, mod, after_ref, mlp_ref):
    mixed = own[...].astype(F32) + other[...].astype(F32)
    after = x_ref[...].astype(F32) + mod[2:3, :] * mixed
    after_ref[...] = after
    mlp_ref[...] = (layer_norm(after) * (1.0 + mod[4:5, :]) + mod[3:4, :]).astype(BF16)


def mlp_input(pair, own, other, modulation):
    return pl.pallas_call(
        mlp_in_kernel,
        out_shape=[
            jax.ShapeDtypeStruct(pair.shape, F32),
            jax.ShapeDtypeStruct(pair.shape, BF16),
        ],
        in_specs=[VMEM] * 4,
        out_specs=[VMEM] * 2,
        name="mlp_input",
    )(pair, own, other, modulation)


def mlp_kernel(x0, x1, x2, x3, w_up, w_down, mod, part0, part1, part2, part3, gathered):
    for k, block in enumerate((x0, x1, x2, x3)):
        gathered[k * PAIR : (k + 1) * PAIR, :] = block[...]
    lifted = jnp.dot(gathered[...], w_up[...], preferred_element_type=F32)
    hidden = jax.nn.gelu(lifted, approximate=True).astype(BF16)
    lowered = lax.dot_general(hidden, w_down[...], NT, preferred_element_type=F32) * mod[5:6, :]
    for k, part in enumerate((part0, part1, part2, part3)):
        part[...] = lowered[k * PAIR : (k + 1) * PAIR].astype(BF16)


def mlp(blocks, w_up, w_down, modulation):
    shape = blocks[0].shape
    return pl.pallas_call(
        mlp_kernel,
        out_shape=[jax.ShapeDtypeStruct(shape, BF16)] * COLUMNS,
        in_specs=[VMEM] * 7,
        out_specs=[VMEM] * COLUMNS,
        scratch_shapes=[pltpu.VMEM((PATCH_TOK, shape[1]), BF16)],
        compiler_params=pltpu.CompilerParams(vmem_limit_bytes=40 * 2**20),
        cost_estimate=pl.CostEstimate(
            flops=10**9, bytes_accessed=5 * 10**6, transcendentals=2 * 10**5
        ),
        name="mlp",
    )(*blocks, w_up, w_down, modulation)


def summed(blocks):
    return sum(block.astype(F32) for block in blocks)


def gather_columns(pair):
    return [pair] + [to_column(pair, -k) for k in range(1, COLUMNS)]


def local(
    carry_x,
    kv_buffer,
    qkv_weight,
    out_weight,
    up_weight,
    down_weight,
    time_table,
    block_table,
    time_index,
    patch_order,
):
    section_index = lax.axis_index("section")
    head_index = lax.axis_index("head")
    column = head_index // 2
    row = head_index % 2
    chosen = jnp.arange(STEPS) == time_index[0]
    modulation = (
        jnp.sum(jnp.where(chosen[:, None, None], time_table, jnp.float32(0.0)), axis=0)
        + block_table[0]
    )
    patches = jnp.stack([patch_of(patch_order, section_index, m) for m in range(MICRO)]).astype(
        jnp.int32
    )
    own = carry_x[0]
    partner = swap_rows(own)
    pair = jnp.where(
        row == 0, jnp.concatenate([own, partner]), jnp.concatenate([partner, own])
    )
    fresh_list = []
    for micro in range(MICRO):
        fresh, *parts = attention(
            micro,
            patches,
            gather_columns(pair),
            modulation,
            qkv_weight[0],
            out_weight[0],
            kv_buffer[0],
            fresh_list[0] if micro else None,
        )
        fresh_list.append(fresh)
        row_sum = summed(
            [parts[0]] + [to_column(parts[k], k) for k in range(1, COLUMNS)]
        ).astype(BF16)
        after_attn, mlp_in = mlp_input(pair, row_sum, swap_rows(row_sum), modulation)
        parts = mlp(gather_columns(mlp_in), up_weight[0], down_weight[0], modulation)
        residual = to_section(after_attn, 0)
        row_sum = summed([to_section(parts[k], k) for k in range(COLUMNS)])
        if micro + 1 < MICRO:
            row_sum = row_sum.astype(BF16)
            both = row_sum.astype(F32) + swap_rows(row_sum).astype(F32)
            pair = (residual + both).astype(BF16)
        else:
            mine = jnp.where(row == 0, row_sum[:HALF], row_sum[HALF:])
            theirs = jnp.where(row == 0, row_sum[HALF:], row_sum[:HALF]).astype(BF16)
            kept = jnp.where(row == 0, residual[:HALF], residual[HALF:])
            outgoing = (kept + (mine + swap_rows(theirs).astype(F32))).astype(BF16)
    rotated = jnp.stack(fresh_list)
    rotated = jnp.concatenate([rotated, rotated], axis=-1)
    begin = ((COLUMNS - column) % COLUMNS) * PAIR
    fresh_kv = lax.dynamic_slice_in_dim(rotated, begin, PATCH_TOK, axis=-1)
    return (outgoing[None], fresh_kv[None])


def solution(mesh):
    placed = (
        P("section", "head", None),
        P("section", None, "head", None),
        P("section", None, "head", None),
        P("section", "head", None),
        P("section", None, "head"),
        P("section", None, "head"),
        P(),
        P("section", None, None),
        P("section"),
        P(),
    )
    return jax.shard_map(
        local,
        mesh=mesh,
        in_specs=placed,
        out_specs=(P("section", "head", None), P("section", None, None, "head", None)),
        check_vma=False,
    )
```

```python
import functools
import math

import jax
import jax.numpy as jnp
from jax import lax
from jax.experimental import pallas as pl
from jax.experimental.pallas import tpu as pltpu
from jax.sharding import PartitionSpec as P

HEAD_DIM = 72
PATCHES = 16
PATCH_TOK = 384
MICRO = 2
STEPS = 20
COLUMNS = 4
SECTIONS = 32
PAIR = PATCH_TOK // COLUMNS
HALF = PAIR // 2
LOG2_SCALE = math.log2(math.e) / math.sqrt(HEAD_DIM)
NT = (((1,), (1,)), ((), ()))
TN = (((0,), (0,)), ((), ()))
F32 = jnp.float32
BF16 = jnp.bfloat16
VMEM = pl.BlockSpec(memory_space=pltpu.VMEM)
SMEM = pl.BlockSpec(memory_space=pltpu.SMEM)
HBM = pl.BlockSpec(memory_space=pltpu.HBM)


def head_of(column, row):
    return (column % COLUMNS) * 2 + row % 2


def flat(section, head):
    return (section % SECTIONS) * 8 + head


ROW_SWAP = [(head_of(c, r), head_of(c, r + 1)) for c in range(COLUMNS) for r in range(2)]


def column_step(step):
    return [(head_of(c, r), head_of(c + step, r)) for c in range(COLUMNS) for r in range(2)]


def section_step(step):
    return [
        (flat(s, head_of(c, r)), flat(s + 1, head_of(c + step, r + (s % 8 == 7))))
        for s in range(SECTIONS)
        for c in range(COLUMNS)
        for r in range(2)
    ]


def swap_rows(value):
    return lax.ppermute(value, "head", ROW_SWAP)


def to_column(value, step):
    return lax.ppermute(value, "head", column_step(step))


def to_section(value, step):
    return lax.ppermute(value, ("section", "head"), section_step(step))


def layer_norm(values_in):
    center = values_in - jnp.mean(values_in, axis=-1, keepdims=True)
    spread = jnp.mean(center * center, axis=-1, keepdims=True)
    return center * lax.rsqrt(spread + 1e-06)


def patch_of(patch_order, section_index, micro):
    position = (micro - section_index) % PATCHES
    picked = jnp.where(jnp.arange(PATCHES) == position, patch_order, 0)
    return jnp.sum(picked)


def place(column, row, k, size, partner):
    offset = ((column + k) % COLUMNS) * PAIR
    if size == HALF:
        offset = offset + ((row + partner) % 2) * HALF
    return pl.multiple_of(offset, HALF)


def patch_copies(blocks, target, column, row, sem):
    size = blocks[0].shape[0]
    return [
        pltpu.make_async_copy(
            block,
            target.at[pl.ds(place(column, row, n % COLUMNS, size, n // COLUMNS), size)],
            sem,
        )
        for n, block in enumerate(blocks)
    ]


def attention_kernel(micro, count, where_ref, *refs):
    blocks, refs = refs[:count], refs[count:]
    mod, weights_hbm, cache, *rest = refs
    if micro:
        earlier, rest = rest[0], rest[1:]
    fresh, attended_ref, inputs, w_qkv, keys, values, queries, scores, result, sem = rest
    width = w_qkv.shape[1]
    column, row = where_ref[2], where_ref[3]
    block_copies = patch_copies(blocks, inputs, column, row, sem.at[0])
    weight_copy = pltpu.make_async_copy(weights_hbm, w_qkv, sem.at[1])
    cache_copies = [
        pltpu.make_async_copy(
            cache.at[0, :, pl.ds(c * PATCH_TOK, PATCH_TOK)], keys.at[c], sem.at[2]
        )
        for c in range(PATCHES)
    ] + [
        pltpu.make_async_copy(
            cache.at[1, :, pl.ds(c * PATCH_TOK, PATCH_TOK)],
            values.at[c, pl.ds(0, width)],
            sem.at[2],
        )
        for c in range(PATCHES)
    ]
    for copy in block_copies + [weight_copy] + cache_copies:
        copy.start()
    values[:, width : width + 16, :] = jnp.ones((PATCHES, 16, PATCH_TOK), BF16)
    for copy in block_copies:
        copy.wait()
    normed = (
        layer_norm(inputs[...].astype(F32)) * (1.0 + mod[1:2, :]) + mod[0:1, :]
    ).astype(BF16)
    weight_copy.wait()
    projected = lax.dot_general(normed, w_qkv[0], NT, preferred_element_type=F32) * LOG2_SCALE
    first_head = lax.broadcasted_iota(jnp.int32, (PATCH_TOK, width), 1) < HEAD_DIM
    queries[0:PATCH_TOK, :] = jnp.where(first_head, projected, 0.0).astype(BF16)
    queries[PATCH_TOK : 2 * PATCH_TOK, :] = jnp.where(first_head, 0.0, projected).astype(BF16)
    new_keys = lax.dot_general(w_qkv[1], normed, NT, preferred_element_type=F32).astype(BF16)
    new_values = lax.dot_general(w_qkv[2], normed, NT, preferred_element_type=F32).astype(BF16)
    fresh[0] = new_keys
    fresh[1] = new_values
    for copy in cache_copies:
        copy.wait()
    if micro:
        keys[where_ref[0]] = earlier[0]
        values[where_ref[0], 0:width] = earlier[1]
    keys[where_ref[micro]] = new_keys
    values[where_ref[micro], 0:width] = new_values
    offset = None
    for part in range(3):
        highest = total = None
        for c in range(PATCHES):
            if part < 2:
                rows = slice(part * PATCH_TOK, (part + 1) * PATCH_TOK)
                block = jnp.dot(queries[rows, :], keys[c], preferred_element_type=F32)
                scores[part, c] = block
                top = jnp.maximum(
                    jnp.maximum(block[:, 0:128], block[:, 128:256]), block[:, 256:384]
                )
                highest = top if highest is None else jnp.maximum(highest, top)
            if part > 0:
                weights = jnp.exp2(scores[part - 1, c] - offset).astype(BF16)
                product = lax.dot_general(weights, values[c], NT, preferred_element_type=F32)
                total = product if total is None else total + product
        if part > 0:
            result[part - 1] = total
        if part < 2:
            offset = jnp.max(highest, axis=1, keepdims=True)
    one = result[0, :, 0:width] / result[0, :, width : width + 1]
    two = result[1, :, 0:width] / result[1, :, width : width + 1]
    attended_ref[...] = jnp.where(first_head, one, two).T.astype(BF16)


def attention(micro, where, blocks, modulation, w_qkv, cache, earlier):
    width, model = w_qkv.shape[1], w_qkv.shape[2]
    extra = [earlier] if micro else []
    return pl.pallas_call(
        functools.partial(attention_kernel, micro, len(blocks)),
        out_shape=[
            jax.ShapeDtypeStruct((2, width, PATCH_TOK), BF16),
            jax.ShapeDtypeStruct((width, PATCH_TOK), BF16),
        ],
        in_specs=[SMEM] + [HBM] * len(blocks) + [VMEM] + [HBM] * 2 + [VMEM] * len(extra),
        out_specs=[VMEM] * 2,
        scratch_shapes=[
            pltpu.VMEM((PATCH_TOK, model), BF16),
            pltpu.VMEM(w_qkv.shape, BF16),
            pltpu.VMEM((PATCHES, width, PATCH_TOK), BF16),
            pltpu.VMEM((PATCHES, width + 16, PATCH_TOK), BF16),
            pltpu.VMEM((2 * PATCH_TOK, width), BF16),
            pltpu.VMEM((2, PATCHES, PATCH_TOK, PATCH_TOK), F32),
            pltpu.VMEM((2, PATCH_TOK, width + 16), F32),
            pltpu.SemaphoreType.DMA((3,)),
        ],
        compiler_params=pltpu.CompilerParams(vmem_limit_bytes=60 * 2**20),
        cost_estimate=pl.CostEstimate(
            flops=4 * 10**9, bytes_accessed=8 * 10**6, transcendentals=5 * 10**6
        ),
        name="attention",
    )(where, *blocks, modulation, w_qkv, cache, *extra)


def mlp_kernel(count, where_ref, *refs):
    blocks, refs = refs[:count], refs[count:]
    heads, refs = refs[:8], refs[8:]
    outs, refs = refs[:8], refs[8:]
    up_hbm, down_hbm, mod, *refs = refs
    parts, refs = refs[:COLUMNS], refs[COLUMNS:]
    inputs, attended, w_out, w_up, w_down, after, lowered, sem = refs
    column, row = where_ref[2], where_ref[3]
    width = heads[0].shape[0]
    out_copies = [
        pltpu.make_async_copy(block, whole.at[pl.ds(n * width, width)], sem.at[0])
        for whole, from_all in ((attended, heads), (w_out, outs))
        for n, block in enumerate(from_all)
    ]
    block_copies = patch_copies(blocks, inputs, column, row, sem.at[1])
    up_copy = pltpu.make_async_copy(up_hbm, w_up, sem.at[2])
    down_copy = pltpu.make_async_copy(down_hbm, w_down, sem.at[3])
    for copy in out_copies + block_copies + [up_copy, down_copy]:
        copy.start()
    for copy in out_copies:
        copy.wait()
    mixed = lax.dot_general(attended[...], w_out[...], TN, preferred_element_type=F32)
    for copy in block_copies:
        copy.wait()
    after_attn = inputs[...].astype(F32) + mod[2:3, :] * mixed
    after[...] = after_attn
    mlp_in = (layer_norm(after_attn) * (1.0 + mod[4:5, :]) + mod[3:4, :]).astype(BF16)
    up_copy.wait()
    lifted = lax.dot_general(mlp_in, w_up[...], NT, preferred_element_type=F32)
    hidden = jax.nn.gelu(lifted, approximate=True).astype(BF16)
    down_copy.wait()
    lowered[...] = jnp.dot(hidden, w_down[...], preferred_element_type=F32) * mod[5:6, :]
    own = pl.ds(place(column, row, 0, HALF, 0), HALF)
    lowered[own, :] = lowered[own, :] + after[own, :]
    for k in range(COLUMNS):
        parts[k][...] = lowered[pl.ds(place(column, row, k, PAIR, 0), PAIR), :].astype(BF16)


def mlp(where, blocks, heads, outs, w_up, w_down, modulation):
    model = w_up.shape[1]
    return pl.pallas_call(
        functools.partial(mlp_kernel, len(blocks)),
        out_shape=[jax.ShapeDtypeStruct((PAIR, model), BF16)] * COLUMNS,
        in_specs=[SMEM] + [HBM] * (len(blocks) + 18) + [VMEM],
        out_specs=[VMEM] * COLUMNS,
        scratch_shapes=[
            pltpu.VMEM((PATCH_TOK, model), BF16),
            pltpu.VMEM((model, PATCH_TOK), BF16),
            pltpu.VMEM((model, model), BF16),
            pltpu.VMEM(w_up.shape, BF16),
            pltpu.VMEM(w_down.shape, BF16),
            pltpu.VMEM((PATCH_TOK, model), F32),
            pltpu.VMEM((PATCH_TOK, model), F32),
            pltpu.SemaphoreType.DMA((4,)),
        ],
        compiler_params=pltpu.CompilerParams(vmem_limit_bytes=60 * 2**20),
        cost_estimate=pl.CostEstimate(
            flops=2 * 10**9, bytes_accessed=8 * 10**6, transcendentals=2 * 10**5
        ),
        name="mlp",
    )(where, *blocks, *heads, *outs, w_up, w_down, modulation)


def summed(blocks):
    return sum(block.astype(F32) for block in blocks)


def gather_columns(block):
    return [block] + [to_column(block, -k) for k in range(1, COLUMNS)]


def gather_heads(block):
    own = gather_columns(block)
    return own + gather_columns(swap_rows(block))


def local(
    carry_x,
    kv_buffer,
    qkv_weight,
    out_weight,
    up_weight,
    down_weight,
    time_table,
    block_table,
    time_index,
    patch_order,
):
    section_index = lax.axis_index("section")
    head_index = lax.axis_index("head")
    column = head_index // 2
    row = head_index % 2
    chosen = jnp.arange(STEPS) == time_index[0]
    modulation = (
        jnp.sum(jnp.where(chosen[:, None, None], time_table, jnp.float32(0.0)), axis=0)
        + block_table[0]
    )
    patches = [patch_of(patch_order, section_index, m) for m in range(MICRO)]
    where = jnp.stack([*patches, column, row]).astype(jnp.int32)
    inputs, w_out = carry_x[0], out_weight[0]
    own_outs = [w_out, to_column(w_out, -1), None, to_column(w_out, -3)]
    own_blocks, partner, w_out = lax.optimization_barrier(
        (gather_columns(inputs), swap_rows(inputs), w_out)
    )
    blocks, own_outs, w_out, partner_out = lax.optimization_barrier(
        (own_blocks + gather_columns(partner), own_outs, w_out, swap_rows(w_out))
    )
    own_outs[2] = to_column(w_out, -2)
    outs = own_outs + gather_columns(partner_out)
    fresh_list = []
    for micro in range(MICRO):
        fresh, attended = attention(
            micro,
            where,
            blocks,
            modulation,
            qkv_weight[0],
            kv_buffer[0],
            fresh_list[0] if micro else None,
        )
        fresh_list.append(fresh)
        if micro == 0:
            attended, outs = lax.optimization_barrier((attended, outs))
        parts = mlp(
            where,
            blocks,
            gather_heads(attended),
            outs,
            up_weight[0].T,
            down_weight[0].T,
            modulation,
        )
        row_sum = summed([to_section(parts[k], k) for k in range(COLUMNS)])
        if micro + 1 < MICRO:
            row_sum = row_sum.astype(BF16)
            both = row_sum.astype(F32) + swap_rows(row_sum).astype(F32)
            blocks = gather_columns(both.astype(BF16))
        else:
            mine = jnp.where(row == 0, row_sum[:HALF], row_sum[HALF:])
            theirs = jnp.where(row == 0, row_sum[HALF:], row_sum[:HALF]).astype(BF16)
            outgoing = (mine + swap_rows(theirs).astype(F32)).astype(BF16)
    return (outgoing[None], jnp.stack(fresh_list)[None])


def solution(mesh):
    placed = (
        P("section", "head", None),
        P("section", None, "head", None),
        P("section", None, "head", None),
        P("section", "head", None),
        P("section", None, "head"),
        P("section", None, "head"),
        P(),
        P("section", None, None),
        P("section"),
        P(),
    )
    return jax.shard_map(
        local,
        mesh=mesh,
        in_specs=placed,
        out_specs=(P("section", "head", None), P("section", None, None, "head", None)),
        check_vma=False,
    )
```

```python
import functools
import math

import jax
import jax.numpy as jnp
from jax import lax
from jax.experimental import pallas as pl
from jax.experimental.pallas import tpu as pltpu
from jax.sharding import PartitionSpec as P

HEAD_DIM = 72
PATCHES = 16
PATCH_TOK = 384
MICRO = 2
STEPS = 20
COLUMNS = 4
SECTIONS = 32
PAIR = PATCH_TOK // COLUMNS
HALF = PAIR // 2
FIRST_COLUMNS = (1, 2, 3)
LATER_COLUMNS = (0,)
LOG2_SCALE = math.log2(math.e) / math.sqrt(HEAD_DIM)
NT = (((1,), (1,)), ((), ()))
F32 = jnp.float32
BF16 = jnp.bfloat16
VMEM = pl.BlockSpec(memory_space=pltpu.VMEM)
SMEM = pl.BlockSpec(memory_space=pltpu.SMEM)
HBM = pl.BlockSpec(memory_space=pltpu.HBM)


def head_of(column, row):
    return (column % COLUMNS) * 2 + row % 2


def flat(section, head):
    return (section % SECTIONS) * 8 + head


ROW_SWAP = [(head_of(c, r), head_of(c, r + 1)) for c in range(COLUMNS) for r in range(2)]


def column_step(step):
    return [(head_of(c, r), head_of(c + step, r)) for c in range(COLUMNS) for r in range(2)]


def section_step(step):
    return [
        (flat(s, head_of(c, r)), flat(s + 1, head_of(c + step, r + (s % 8 == 7))))
        for s in range(SECTIONS)
        for c in range(COLUMNS)
        for r in range(2)
    ]


def swap_rows(value):
    return lax.ppermute(value, "head", ROW_SWAP)


def to_column(value, step):
    return lax.ppermute(value, "head", column_step(step))


def to_section(value, step):
    return lax.ppermute(value, ("section", "head"), section_step(step))


def layer_norm(values_in):
    center = values_in - jnp.mean(values_in, axis=-1, keepdims=True)
    spread = jnp.mean(center * center, axis=-1, keepdims=True)
    return center * lax.rsqrt(spread + 1e-06)


def patch_of(patch_order, section_index, micro):
    position = (micro - section_index) % PATCHES
    picked = jnp.where(jnp.arange(PATCHES) == position, patch_order, 0)
    return jnp.sum(picked)


def place(column, row, k, size, partner):
    offset = ((column + k) % COLUMNS) * PAIR
    if size == HALF:
        offset = offset + ((row + partner) % 2) * HALF
    return pl.multiple_of(offset, HALF)


def patch_copies(blocks, target, column, row, sem):
    size = blocks[0].shape[0]
    return [
        pltpu.make_async_copy(
            block,
            target.at[pl.ds(place(column, row, n % COLUMNS, size, n // COLUMNS), size)],
            sem,
        )
        for n, block in enumerate(blocks)
    ]


def attend(queries, keys, values, w_out, scores, result, parts):
    width, rows = w_out.shape[0], queries.shape[1]
    offset = None
    for stage in range(3):
        highest = total = None
        for c in range(PATCHES):
            tokens = slice(c * PATCH_TOK, (c + 1) * PATCH_TOK)
            if stage < 2:
                block = jnp.dot(queries[stage], keys[:, tokens], preferred_element_type=F32)
                scores[stage, c] = block
                top = jnp.maximum(
                    jnp.maximum(block[:, 0:128], block[:, 128:256]), block[:, 256:384]
                )
                highest = top if highest is None else jnp.maximum(highest, top)
            if stage > 0:
                weights = jnp.exp2(scores[stage - 1, c] - offset).astype(BF16)
                product = lax.dot_general(
                    weights, values[:, tokens], NT, preferred_element_type=F32
                )
                total = product if total is None else total + product
        if stage > 0:
            result[stage - 1] = total
        if stage < 2:
            offset = jnp.max(highest, axis=1, keepdims=True)
    one = result[0, :, 0:width] / result[0, :, width : width + 1]
    two = result[1, :, 0:width] / result[1, :, width : width + 1]
    first_head = lax.broadcasted_iota(jnp.int32, (rows, width), 1) < HEAD_DIM
    attended = jnp.where(first_head, one, two).astype(BF16)
    mixed = jnp.dot(attended, w_out[...], preferred_element_type=F32).astype(BF16)
    for n, part in enumerate(parts):
        part[...] = mixed[n * PAIR : (n + 1) * PAIR]


def first_kernel(micro, count, where_ref, *refs):
    blocks, refs = refs[:count], refs[count:]
    mod, qkv_hbm, out_hbm, cache, *rest = refs
    if micro:
        earlier, rest = rest[0], rest[1:]
    fresh, part_1, part_2, part_3, later, keys, values, *rest = rest
    inputs, w_qkv, w_out, projected, queries, scores, result, sem = rest
    width = w_qkv.shape[1]
    column, row = where_ref[2], where_ref[3]
    block_copies = patch_copies(blocks, inputs, column, row, sem.at[0])
    qkv_copy = pltpu.make_async_copy(qkv_hbm, w_qkv, sem.at[1])
    cache_copies = [
        pltpu.make_async_copy(cache.at[0], keys, sem.at[2]),
        pltpu.make_async_copy(cache.at[1], values.at[pl.ds(0, width)], sem.at[3]),
    ]
    out_copy = pltpu.make_async_copy(out_hbm, w_out, sem.at[4])
    for copy in block_copies + [qkv_copy] + cache_copies + [out_copy]:
        copy.start()
    values[width : width + 16, :] = jnp.ones((16, PATCHES * PATCH_TOK), BF16)
    for copy in block_copies:
        copy.wait()
    normed = (
        layer_norm(inputs[...].astype(F32)) * (1.0 + mod[1:2, :]) + mod[0:1, :]
    ).astype(BF16)
    qkv_copy.wait()
    projected[...] = (
        lax.dot_general(normed, w_qkv[0], NT, preferred_element_type=F32) * LOG2_SCALE
    )
    first_head = lax.broadcasted_iota(jnp.int32, (PAIR, width), 1) < HEAD_DIM
    for target, columns in ((queries, FIRST_COLUMNS), (later, LATER_COLUMNS)):
        for n, k in enumerate(columns):
            rows = projected[pl.ds(place(column, row, k, PAIR, 0), PAIR), :]
            here = slice(n * PAIR, (n + 1) * PAIR)
            target[0, here] = jnp.where(first_head, rows, 0.0).astype(BF16)
            target[1, here] = jnp.where(first_head, 0.0, rows).astype(BF16)
    w_kv = w_qkv[1:3].reshape(2 * width, w_qkv.shape[2])
    new_kv = lax.dot_general(w_kv, normed, NT, preferred_element_type=F32).astype(BF16)
    new_keys, new_values = new_kv[0:width], new_kv[width : 2 * width]
    fresh[0] = new_keys
    fresh[1] = new_values
    for copy in cache_copies:
        copy.wait()
    if micro:
        before = pl.ds(pl.multiple_of(where_ref[0] * PATCH_TOK, PATCH_TOK), PATCH_TOK)
        keys[:, before] = earlier[0]
        values[0:width, before] = earlier[1]
    now = pl.ds(pl.multiple_of(where_ref[micro] * PATCH_TOK, PATCH_TOK), PATCH_TOK)
    keys[:, now] = new_keys
    values[0:width, now] = new_values
    out_copy.wait()
    attend(queries, keys, values, w_out, scores, result, (part_1, part_2, part_3))


def first_columns(micro, where, blocks, modulation, w_qkv, w_out, cache, earlier):
    width, model = w_qkv.shape[1], w_qkv.shape[2]
    tokens = cache.shape[2]
    extra = [earlier] if micro else []
    return pl.pallas_call(
        functools.partial(first_kernel, micro, len(blocks)),
        out_shape=[
            jax.ShapeDtypeStruct((2, width, PATCH_TOK), BF16),
            jax.ShapeDtypeStruct((PAIR, model), BF16),
            jax.ShapeDtypeStruct((PAIR, model), BF16),
            jax.ShapeDtypeStruct((PAIR, model), BF16),
            jax.ShapeDtypeStruct((2, PAIR, width), BF16),
            jax.ShapeDtypeStruct((width, tokens), BF16),
            jax.ShapeDtypeStruct((width + 16, tokens), BF16),
        ],
        in_specs=[SMEM] + [HBM] * len(blocks) + [VMEM] + [HBM] * 3 + [VMEM] * len(extra),
        out_specs=[VMEM] * 7,
        scratch_shapes=[
            pltpu.VMEM((PATCH_TOK, model), BF16),
            pltpu.VMEM(w_qkv.shape, BF16),
            pltpu.VMEM(w_out.shape, BF16),
            pltpu.VMEM((PATCH_TOK, width), F32),
            pltpu.VMEM((2, 3 * PAIR, width), BF16),
            pltpu.VMEM((2, PATCHES, 3 * PAIR, PATCH_TOK), F32),
            pltpu.VMEM((2, 3 * PAIR, width + 16), F32),
            pltpu.SemaphoreType.DMA((5,)),
        ],
        compiler_params=pltpu.CompilerParams(vmem_limit_bytes=56 * 2**20),
        cost_estimate=pl.CostEstimate(
            flops=3 * 10**9, bytes_accessed=7 * 10**6, transcendentals=2 * 10**6
        ),
        name="first_columns",
    )(where, *blocks, modulation, w_qkv, w_out, cache, *extra)


def later_kernel(queries, keys, values, w_out, part, scores, result):
    attend(queries, keys, values, w_out, scores, result, (part,))


def later_columns(queries, keys, values, w_out):
    width, model = w_out.shape
    return pl.pallas_call(
        later_kernel,
        out_shape=jax.ShapeDtypeStruct((PAIR, model), BF16),
        in_specs=[VMEM] * 4,
        out_specs=VMEM,
        scratch_shapes=[
            pltpu.VMEM((2, PATCHES, PAIR, PATCH_TOK), F32),
            pltpu.VMEM((2, PAIR, width + 16), F32),
        ],
        compiler_params=pltpu.CompilerParams(vmem_limit_bytes=24 * 2**20),
        cost_estimate=pl.CostEstimate(
            flops=3 * 10**9, bytes_accessed=10**6, transcendentals=2 * 10**6
        ),
        name="later_columns",
    )(queries, keys, values, w_out)


def mlp_input_kernel(count, where_ref, *refs):
    blocks, (own, other, mod, after_ref, mlp_ref, pair) = refs[:count], refs[count:]
    size = blocks[0].shape[0]
    for n, block in enumerate(blocks):
        first = pl.multiple_of(((where_ref[3] + n) % 2) * HALF, HALF) if count > 1 else 0
        pair[pl.ds(first, size), :] = block[...].astype(F32)
    mixed = own[...].astype(F32) + other[...].astype(F32)
    after = pair[...] + mod[2:3, :] * mixed
    after_ref[...] = after
    mlp_ref[...] = (layer_norm(after) * (1.0 + mod[4:5, :]) + mod[3:4, :]).astype(BF16)


def mlp_input(where, blocks, own, other, modulation):
    return pl.pallas_call(
        functools.partial(mlp_input_kernel, len(blocks)),
        out_shape=[
            jax.ShapeDtypeStruct(own.shape, F32),
            jax.ShapeDtypeStruct(own.shape, BF16),
        ],
        in_specs=[SMEM] + [VMEM] * (len(blocks) + 3),
        out_specs=[VMEM] * 2,
        scratch_shapes=[pltpu.VMEM(own.shape, F32)],
        compiler_params=pltpu.CompilerParams(vmem_limit_bytes=24 * 2**20),
        name="mlp_input",
    )(where, *blocks, own, other, modulation)


def mlp_kernel(has_residual, where_ref, block, w_up, w_down, mod, *refs):
    lifted = lax.dot_general(block[...], w_up[...], NT, preferred_element_type=F32)
    hidden = jax.nn.gelu(lifted, approximate=True).astype(BF16)
    lowered = jnp.dot(hidden, w_down[...], preferred_element_type=F32) * mod[5:6, :]
    if has_residual:
        half = lax.broadcasted_iota(jnp.int32, (PAIR, 1), 0) // HALF
        lowered = lowered + jnp.where(half == where_ref[3], refs[0][...], 0.0)
    refs[-1][...] = lowered.astype(BF16)


def mlp(where, block, w_up, w_down, modulation, after=None):
    extra = [] if after is None else [after]
    return pl.pallas_call(
        functools.partial(mlp_kernel, after is not None),
        out_shape=jax.ShapeDtypeStruct(block.shape, BF16),
        in_specs=[SMEM] + [VMEM] * (4 + len(extra)),
        out_specs=VMEM,
        compiler_params=pltpu.CompilerParams(vmem_limit_bytes=24 * 2**20),
        cost_estimate=pl.CostEstimate(
            flops=10**9, bytes_accessed=10**6, transcendentals=10**5
        ),
        name="mlp",
    )(where, block, w_up, w_down, modulation, *extra)


def summed(blocks):
    return sum(block.astype(F32) for block in blocks)


def gather_columns(block):
    return [block] + [to_column(block, -k) for k in range(1, COLUMNS)]


def gather_heads(block):
    own = gather_columns(block)
    return own + gather_columns(swap_rows(block))


def local(
    carry_x,
    kv_buffer,
    qkv_weight,
    out_weight,
    up_weight,
    down_weight,
    time_table,
    block_table,
    time_index,
    patch_order,
):
    section_index = lax.axis_index("section")
    head_index = lax.axis_index("head")
    column = head_index // 2
    row = head_index % 2
    chosen = jnp.arange(STEPS) == time_index[0]
    modulation = (
        jnp.sum(jnp.where(chosen[:, None, None], time_table, jnp.float32(0.0)), axis=0)
        + block_table[0]
    )
    patches = [patch_of(patch_order, section_index, m) for m in range(MICRO)]
    where = jnp.stack([*patches, column, row]).astype(jnp.int32)
    w_qkv, cache, w_out = qkv_weight[0], kv_buffer[0], out_weight[0]
    w_up, w_down = up_weight[0].T, down_weight[0].T
    blocks = gather_heads(carry_x[0])
    fresh_list = []
    for micro in range(MICRO):
        earlier = fresh_list[0] if micro else None
        fresh, *parts = first_columns(
            micro, where, blocks, modulation, w_qkv, w_out, cache, earlier
        )
        fresh_list.append(fresh)
        mine = later_columns(*parts[3:], w_out)
        row_sum = summed([mine] + [to_column(parts[k - 1], k) for k in (1, 2, 3)]).astype(BF16)
        pair = [blocks[0]] if micro else [blocks[0], blocks[COLUMNS]]
        after, mlp_in = mlp_input(where, pair, row_sum, swap_rows(row_sum), modulation)
        gathered = gather_columns(mlp_in)
        parts = [mlp(where, mlp_in, w_up, w_down, modulation, after)] + [
            mlp(where, gathered[k], w_up, w_down, modulation) for k in range(1, COLUMNS)
        ]
        row_sum = summed([to_section(parts[k], k) for k in range(COLUMNS)])
        if micro + 1 < MICRO:
            row_sum = row_sum.astype(BF16)
            both = row_sum.astype(F32) + swap_rows(row_sum).astype(F32)
            blocks = gather_columns(both.astype(BF16))
        else:
            mine = jnp.where(row == 0, row_sum[:HALF], row_sum[HALF:])
            theirs = jnp.where(row == 0, row_sum[HALF:], row_sum[:HALF]).astype(BF16)
            outgoing = (mine + swap_rows(theirs).astype(F32)).astype(BF16)
    return (outgoing[None], jnp.stack(fresh_list)[None])


def solution(mesh):
    placed = (
        P("section", "head", None),
        P("section", None, "head", None),
        P("section", None, "head", None),
        P("section", "head", None),
        P("section", None, "head"),
        P("section", None, "head"),
        P(),
        P("section", None, None),
        P("section"),
        P(),
    )
    return jax.shard_map(
        local,
        mesh=mesh,
        in_specs=placed,
        out_specs=(P("section", "head", None), P("section", None, None, "head", None)),
        check_vma=False,
    )
```

```python
import functools
import math

import jax
import jax.numpy as jnp
from jax import lax
from jax.experimental import pallas as pl
from jax.experimental.pallas import tpu as pltpu
from jax.sharding import PartitionSpec as P

HEAD_DIM = 72
PATCHES = 16
PATCH_TOK = 384
MICRO = 2
STEPS = 20
COLUMNS = 4
SECTIONS = 32
PAIR = PATCH_TOK // COLUMNS
HALF = PAIR // 2
CHUNK = 3072
FIRST_COLUMNS = (1, 2, 3)
LATER_COLUMNS = (0,)
LOG2_SCALE = math.log2(math.e) / math.sqrt(HEAD_DIM)
NT = (((1,), (1,)), ((), ()))
F32 = jnp.float32
BF16 = jnp.bfloat16
VMEM = pl.BlockSpec(memory_space=pltpu.VMEM)
SMEM = pl.BlockSpec(memory_space=pltpu.SMEM)
HBM = pl.BlockSpec(memory_space=pltpu.HBM)


def head_of(column, row):
    return (column % COLUMNS) * 2 + row % 2


def flat(section, head):
    return (section % SECTIONS) * 8 + head


ROW_SWAP = [(head_of(c, r), head_of(c, r + 1)) for c in range(COLUMNS) for r in range(2)]


def column_step(step):
    return [(head_of(c, r), head_of(c + step, r)) for c in range(COLUMNS) for r in range(2)]


def section_step(step):
    return [
        (flat(s, head_of(c, r)), flat(s + 1, head_of(c + step, r + (s % 8 == 7))))
        for s in range(SECTIONS)
        for c in range(COLUMNS)
        for r in range(2)
    ]


def swap_rows(value):
    return lax.ppermute(value, "head", ROW_SWAP)


def to_column(value, step):
    return lax.ppermute(value, "head", column_step(step))


def to_section(value, step):
    return lax.ppermute(value, ("section", "head"), section_step(step))


def layer_norm(values_in):
    center = values_in - jnp.mean(values_in, axis=-1, keepdims=True)
    spread = jnp.mean(center * center, axis=-1, keepdims=True)
    return center * lax.rsqrt(spread + 1e-06)


def patch_of(patch_order, section_index, micro):
    position = (micro - section_index) % PATCHES
    picked = jnp.where(jnp.arange(PATCHES) == position, patch_order, 0)
    return jnp.sum(picked)


def place(column, row, k, size, partner):
    offset = ((column + k) % COLUMNS) * PAIR
    if size == HALF:
        offset = offset + ((row + partner) % 2) * HALF
    return pl.multiple_of(offset, HALF)


def patch_copies(blocks, target, column, row, sem):
    size = blocks[0].shape[0]
    return [
        pltpu.make_async_copy(
            block,
            target.at[pl.ds(place(column, row, n % COLUMNS, size, n // COLUMNS), size)],
            sem,
        )
        for n, block in enumerate(blocks)
    ]


def attend(queries, keys, values, w_out, scores, result, parts):
    width, rows = w_out.shape[0], queries.shape[1]
    offset = None
    for stage in range(3):
        highest = total = None
        for c in range(keys.shape[1] // CHUNK):
            tokens = slice(c * CHUNK, (c + 1) * CHUNK)
            if stage < 2:
                block = jnp.dot(queries[stage], keys[:, tokens], preferred_element_type=F32)
                scores[stage, c] = block
                for lane in range(0, CHUNK, 128):
                    top = block[:, lane : lane + 128]
                    highest = top if highest is None else jnp.maximum(highest, top)
            if stage > 0:
                weights = jnp.exp2(scores[stage - 1, c] - offset).astype(BF16)
                product = lax.dot_general(
                    weights, values[:, tokens], NT, preferred_element_type=F32
                )
                total = product if total is None else total + product
        if stage > 0:
            result[stage - 1] = total
        if stage < 2:
            offset = jnp.max(highest, axis=1, keepdims=True)
    one = result[0, :, 0:width] / result[0, :, width : width + 1]
    two = result[1, :, 0:width] / result[1, :, width : width + 1]
    first_head = lax.broadcasted_iota(jnp.int32, (rows, width), 1) < HEAD_DIM
    attended = jnp.where(first_head, one, two).astype(BF16)
    mixed = jnp.dot(attended, w_out[...], preferred_element_type=F32).astype(BF16)
    for n, part in enumerate(parts):
        part[...] = mixed[n * PAIR : (n + 1) * PAIR]


def first_kernel(micro, count, where_ref, *refs):
    blocks, refs = refs[:count], refs[count:]
    mod, qkv_hbm, out_hbm, cache, *rest = refs
    if micro:
        earlier, rest = rest[0], rest[1:]
    fresh, part_1, part_2, part_3, later, keys, values, *rest = rest
    inputs, w_qkv, w_out, projected, queries, scores, result, sem = rest
    width = w_qkv.shape[1]
    column, row = where_ref[2], where_ref[3]
    block_copies = patch_copies(blocks, inputs, column, row, sem.at[0])
    qkv_copy = pltpu.make_async_copy(qkv_hbm, w_qkv, sem.at[1])
    cache_copies = [
        pltpu.make_async_copy(cache.at[0], keys, sem.at[2]),
        pltpu.make_async_copy(cache.at[1], values.at[pl.ds(0, width)], sem.at[3]),
    ]
    out_copy = pltpu.make_async_copy(out_hbm, w_out, sem.at[4])
    for copy in block_copies + [qkv_copy] + cache_copies + [out_copy]:
        copy.start()
    values[width : width + 16, :] = jnp.ones((16, PATCHES * PATCH_TOK), BF16)
    for copy in block_copies:
        copy.wait()
    normed = (
        layer_norm(inputs[...].astype(F32)) * (1.0 + mod[1:2, :]) + mod[0:1, :]
    ).astype(BF16)
    qkv_copy.wait()
    projected[...] = (
        lax.dot_general(normed, w_qkv[0], NT, preferred_element_type=F32) * LOG2_SCALE
    )
    first_head = lax.broadcasted_iota(jnp.int32, (PAIR, width), 1) < HEAD_DIM
    for target, columns in ((queries, FIRST_COLUMNS), (later, LATER_COLUMNS)):
        for n, k in enumerate(columns):
            rows = projected[pl.ds(place(column, row, k, PAIR, 0), PAIR), :]
            here = slice(n * PAIR, (n + 1) * PAIR)
            target[0, here] = jnp.where(first_head, rows, 0.0).astype(BF16)
            target[1, here] = jnp.where(first_head, 0.0, rows).astype(BF16)
    w_kv = w_qkv[1:3].reshape(2 * width, w_qkv.shape[2])
    new_kv = lax.dot_general(w_kv, normed, NT, preferred_element_type=F32).astype(BF16)
    new_keys, new_values = new_kv[0:width], new_kv[width : 2 * width]
    fresh[0] = new_keys
    fresh[1] = new_values
    for copy in cache_copies:
        copy.wait()
    if micro:
        before = pl.ds(pl.multiple_of(where_ref[0] * PATCH_TOK, PATCH_TOK), PATCH_TOK)
        keys[:, before] = earlier[0]
        values[0:width, before] = earlier[1]
    now = pl.ds(pl.multiple_of(where_ref[micro] * PATCH_TOK, PATCH_TOK), PATCH_TOK)
    keys[:, now] = new_keys
    values[0:width, now] = new_values
    out_copy.wait()
    attend(queries, keys, values, w_out, scores, result, (part_1, part_2, part_3))


def first_columns(micro, where, blocks, modulation, w_qkv, w_out, cache, earlier):
    width, model = w_qkv.shape[1], w_qkv.shape[2]
    tokens = cache.shape[2]
    extra = [earlier] if micro else []
    return pl.pallas_call(
        functools.partial(first_kernel, micro, len(blocks)),
        out_shape=[
            jax.ShapeDtypeStruct((2, width, PATCH_TOK), BF16),
            jax.ShapeDtypeStruct((PAIR, model), BF16),
            jax.ShapeDtypeStruct((PAIR, model), BF16),
            jax.ShapeDtypeStruct((PAIR, model), BF16),
            jax.ShapeDtypeStruct((2, PAIR, width), BF16),
            jax.ShapeDtypeStruct((width, tokens), BF16),
            jax.ShapeDtypeStruct((width + 16, tokens), BF16),
        ],
        in_specs=[SMEM] + [HBM] * len(blocks) + [VMEM] + [HBM] * 3 + [VMEM] * len(extra),
        out_specs=[VMEM] * 7,
        scratch_shapes=[
            pltpu.VMEM((PATCH_TOK, model), BF16),
            pltpu.VMEM(w_qkv.shape, BF16),
            pltpu.VMEM(w_out.shape, BF16),
            pltpu.VMEM((PATCH_TOK, width), F32),
            pltpu.VMEM((2, 3 * PAIR, width), BF16),
            pltpu.VMEM((2, tokens // CHUNK, 3 * PAIR, CHUNK), F32),
            pltpu.VMEM((2, 3 * PAIR, width + 16), F32),
            pltpu.SemaphoreType.DMA((5,)),
        ],
        compiler_params=pltpu.CompilerParams(vmem_limit_bytes=56 * 2**20),
        cost_estimate=pl.CostEstimate(
            flops=3 * 10**9, bytes_accessed=7 * 10**6, transcendentals=2 * 10**6
        ),
        name="first_columns",
    )(where, *blocks, modulation, w_qkv, w_out, cache, *extra)


def later_kernel(queries, keys, values, w_out, part, scores, result):
    attend(queries, keys, values, w_out, scores, result, (part,))


def later_columns(queries, keys, values, w_out):
    width, model = w_out.shape
    return pl.pallas_call(
        later_kernel,
        out_shape=jax.ShapeDtypeStruct((PAIR, model), BF16),
        in_specs=[VMEM] * 4,
        out_specs=VMEM,
        scratch_shapes=[
            pltpu.VMEM((2, keys.shape[1] // CHUNK, PAIR, CHUNK), F32),
            pltpu.VMEM((2, PAIR, width + 16), F32),
        ],
        compiler_params=pltpu.CompilerParams(vmem_limit_bytes=24 * 2**20),
        cost_estimate=pl.CostEstimate(
            flops=3 * 10**9, bytes_accessed=10**6, transcendentals=2 * 10**6
        ),
        name="later_columns",
    )(queries, keys, values, w_out)


def mlp_input_kernel(count, where_ref, *refs):
    blocks, (own, other, mod, after_ref, mlp_ref, pair) = refs[:count], refs[count:]
    size = blocks[0].shape[0]
    for n, block in enumerate(blocks):
        first = pl.multiple_of(((where_ref[3] + n) % 2) * HALF, HALF) if count > 1 else 0
        pair[pl.ds(first, size), :] = block[...].astype(F32)
    mixed = own[...].astype(F32) + other[...].astype(F32)
    after = pair[...] + mod[2:3, :] * mixed
    after_ref[...] = after
    mlp_ref[...] = (layer_norm(after) * (1.0 + mod[4:5, :]) + mod[3:4, :]).astype(BF16)


def mlp_input(where, blocks, own, other, modulation):
    return pl.pallas_call(
        functools.partial(mlp_input_kernel, len(blocks)),
        out_shape=[
            jax.ShapeDtypeStruct(own.shape, F32),
            jax.ShapeDtypeStruct(own.shape, BF16),
        ],
        in_specs=[SMEM] + [VMEM] * (len(blocks) + 3),
        out_specs=[VMEM] * 2,
        scratch_shapes=[pltpu.VMEM(own.shape, F32)],
        compiler_params=pltpu.CompilerParams(vmem_limit_bytes=24 * 2**20),
        name="mlp_input",
    )(where, *blocks, own, other, modulation)


def mlp_kernel(has_residual, where_ref, block, w_up, w_down, mod, *refs):
    lifted = lax.dot_general(block[...], w_up[...], NT, preferred_element_type=F32)
    hidden = jax.nn.gelu(lifted, approximate=True).astype(BF16)
    lowered = jnp.dot(hidden, w_down[...], preferred_element_type=F32) * mod[5:6, :]
    if has_residual:
        half = lax.broadcasted_iota(jnp.int32, (PAIR, 1), 0) // HALF
        lowered = lowered + jnp.where(half == where_ref[3], refs[0][...], 0.0)
    refs[-1][...] = lowered.astype(BF16)


def mlp(where, block, w_up, w_down, modulation, after=None):
    extra = [] if after is None else [after]
    return pl.pallas_call(
        functools.partial(mlp_kernel, after is not None),
        out_shape=jax.ShapeDtypeStruct(block.shape, BF16),
        in_specs=[SMEM] + [VMEM] * (4 + len(extra)),
        out_specs=VMEM,
        compiler_params=pltpu.CompilerParams(vmem_limit_bytes=24 * 2**20),
        cost_estimate=pl.CostEstimate(
            flops=10**9, bytes_accessed=10**6, transcendentals=10**5
        ),
        name="mlp",
    )(where, block, w_up, w_down, modulation, *extra)


def summed(blocks):
    return sum(block.astype(F32) for block in blocks)


def gather_columns(block):
    return [block] + [to_column(block, -k) for k in range(1, COLUMNS)]


def gather_heads(block):
    own = gather_columns(block)
    return own + gather_columns(swap_rows(block))


def local(
    carry_x,
    kv_buffer,
    qkv_weight,
    out_weight,
    up_weight,
    down_weight,
    time_table,
    block_table,
    time_index,
    patch_order,
):
    section_index = lax.axis_index("section")
    head_index = lax.axis_index("head")
    column = head_index // 2
    row = head_index % 2
    chosen = jnp.arange(STEPS) == time_index[0]
    modulation = (
        jnp.sum(jnp.where(chosen[:, None, None], time_table, jnp.float32(0.0)), axis=0)
        + block_table[0]
    )
    patches = [patch_of(patch_order, section_index, m) for m in range(MICRO)]
    where = jnp.stack([*patches, column, row]).astype(jnp.int32)
    w_qkv, cache, w_out = qkv_weight[0], kv_buffer[0], out_weight[0]
    w_up, w_down = up_weight[0].T, down_weight[0].T
    blocks = gather_heads(carry_x[0])
    fresh_list = []
    for micro in range(MICRO):
        earlier = fresh_list[0] if micro else None
        fresh, *parts = first_columns(
            micro, where, blocks, modulation, w_qkv, w_out, cache, earlier
        )
        fresh_list.append(fresh)
        mine = later_columns(*parts[3:], w_out)
        row_sum = summed([mine] + [to_column(parts[k - 1], k) for k in (1, 2, 3)]).astype(BF16)
        pair = [blocks[0]] if micro else [blocks[0], blocks[COLUMNS]]
        after, mlp_in = mlp_input(where, pair, row_sum, swap_rows(row_sum), modulation)
        gathered = gather_columns(mlp_in)
        parts = [mlp(where, mlp_in, w_up, w_down, modulation, after)] + [
            mlp(where, gathered[k], w_up, w_down, modulation) for k in range(1, COLUMNS)
        ]
        parts[0] = lax.optimization_barrier(parts)[0]
        row_sum = summed([to_section(parts[k], k) for k in range(COLUMNS)])
        if micro + 1 < MICRO:
            row_sum = row_sum.astype(BF16)
            both = row_sum.astype(F32) + swap_rows(row_sum).astype(F32)
            blocks = gather_columns(both.astype(BF16))
        else:
            mine = jnp.where(row == 0, row_sum[:HALF], row_sum[HALF:])
            theirs = jnp.where(row == 0, row_sum[HALF:], row_sum[:HALF]).astype(BF16)
            outgoing = (mine + swap_rows(theirs).astype(F32)).astype(BF16)
    return (outgoing[None], jnp.stack(fresh_list)[None])


def solution(mesh):
    placed = (
        P("section", "head", None),
        P("section", None, "head", None),
        P("section", None, "head", None),
        P("section", "head", None),
        P("section", None, "head"),
        P("section", None, "head"),
        P(),
        P("section", None, None),
        P("section"),
        P(),
    )
    return jax.shard_map(
        local,
        mesh=mesh,
        in_specs=placed,
        out_specs=(P("section", "head", None), P("section", None, None, "head", None)),
        check_vma=False,
    )
```

```python
import functools
import math

import jax
import jax.numpy as jnp
from jax import lax
from jax.experimental import pallas as pl
from jax.experimental.pallas import tpu as pltpu
from jax.sharding import PartitionSpec as P

HEAD_DIM = 72
PATCHES = 16
PATCH_TOK = 384
MICRO = 2
STEPS = 20
COLUMNS = 4
SECTIONS = 32
PAIR = PATCH_TOK // COLUMNS
HALF = PAIR // 2
CHUNK = 3072
LOG2_SCALE = math.log2(math.e) / math.sqrt(HEAD_DIM)
NT = (((1,), (1,)), ((), ()))
TN = (((0,), (0,)), ((), ()))
F32 = jnp.float32
BF16 = jnp.bfloat16
VMEM = pl.BlockSpec(memory_space=pltpu.VMEM)
SMEM = pl.BlockSpec(memory_space=pltpu.SMEM)
HBM = pl.BlockSpec(memory_space=pltpu.HBM)


def head_of(column, row):
    return (column % COLUMNS) * 2 + row % 2


def flat(section, head):
    return (section % SECTIONS) * 8 + head


ROW_SWAP = [(head_of(c, r), head_of(c, r + 1)) for c in range(COLUMNS) for r in range(2)]


def column_step(step):
    return [(head_of(c, r), head_of(c + step, r)) for c in range(COLUMNS) for r in range(2)]


def section_step(step):
    return [
        (flat(s, head_of(c, r)), flat(s + 1, head_of(c + step, r + (s % 8 == 7))))
        for s in range(SECTIONS)
        for c in range(COLUMNS)
        for r in range(2)
    ]


def swap_rows(value):
    return lax.ppermute(value, "head", ROW_SWAP)


def to_column(value, step):
    return lax.ppermute(value, "head", column_step(step))


def to_section(value, step):
    return lax.ppermute(value, ("section", "head"), section_step(step))


def layer_norm(values_in):
    center = values_in - jnp.mean(values_in, axis=-1, keepdims=True)
    spread = jnp.mean(center * center, axis=-1, keepdims=True)
    return center * lax.rsqrt(spread + 1e-06)


def patch_of(patch_order, section_index, micro):
    position = (micro - section_index) % PATCHES
    picked = jnp.where(jnp.arange(PATCHES) == position, patch_order, 0)
    return jnp.sum(picked)


def place(column, row, k, size, partner):
    offset = ((column + k) % COLUMNS) * PAIR
    if size == HALF:
        offset = offset + ((row + partner) % 2) * HALF
    return pl.multiple_of(offset, HALF)


def patch_copies(blocks, target, column, row, sem):
    size = blocks[0].shape[0]
    return [
        pltpu.make_async_copy(
            block,
            target.at[pl.ds(place(column, row, n % COLUMNS, size, n // COLUMNS), size)],
            sem,
        )
        for n, block in enumerate(blocks)
    ]


def attention_kernel(micro, count, where_ref, *refs):
    blocks, refs = refs[:count], refs[count:]
    mod, weights_hbm, cache, *rest = refs
    if micro:
        earlier, rest = rest[0], rest[1:]
    fresh, attended_ref, inputs, w_qkv, keys, values, queries, scores, result, sem = rest
    width = w_qkv.shape[1]
    column, row = where_ref[2], where_ref[3]
    block_copies = patch_copies(blocks, inputs, column, row, sem.at[0])
    weight_copy = pltpu.make_async_copy(weights_hbm, w_qkv, sem.at[1])
    cache_copies = [
        pltpu.make_async_copy(cache.at[0], keys, sem.at[2]),
        pltpu.make_async_copy(cache.at[1], values.at[pl.ds(0, width)], sem.at[3]),
    ]
    for copy in block_copies + [weight_copy] + cache_copies:
        copy.start()
    values[width : width + 16, :] = jnp.ones((16, PATCHES * PATCH_TOK), BF16)
    for copy in block_copies:
        copy.wait()
    normed = (
        layer_norm(inputs[...].astype(F32)) * (1.0 + mod[1:2, :]) + mod[0:1, :]
    ).astype(BF16)
    weight_copy.wait()
    projected = lax.dot_general(normed, w_qkv[0], NT, preferred_element_type=F32) * LOG2_SCALE
    first_head = lax.broadcasted_iota(jnp.int32, (PATCH_TOK, width), 1) < HEAD_DIM
    queries[0:PATCH_TOK, :] = jnp.where(first_head, projected, 0.0).astype(BF16)
    queries[PATCH_TOK : 2 * PATCH_TOK, :] = jnp.where(first_head, 0.0, projected).astype(BF16)
    w_kv = w_qkv[1:3].reshape(2 * width, w_qkv.shape[2])
    new_kv = lax.dot_general(w_kv, normed, NT, preferred_element_type=F32).astype(BF16)
    new_keys, new_values = new_kv[0:width], new_kv[width : 2 * width]
    fresh[0] = new_keys
    fresh[1] = new_values
    for copy in cache_copies:
        copy.wait()
    if micro:
        before = pl.ds(pl.multiple_of(where_ref[0] * PATCH_TOK, PATCH_TOK), PATCH_TOK)
        keys[:, before] = earlier[0]
        values[0:width, before] = earlier[1]
    now = pl.ds(pl.multiple_of(where_ref[micro] * PATCH_TOK, PATCH_TOK), PATCH_TOK)
    keys[:, now] = new_keys
    values[0:width, now] = new_values
    offset = None
    for part in range(3):
        highest = total = None
        for c in range(keys.shape[1] // CHUNK):
            tokens = slice(c * CHUNK, (c + 1) * CHUNK)
            if part < 2:
                rows = slice(part * PATCH_TOK, (part + 1) * PATCH_TOK)
                block = jnp.dot(queries[rows, :], keys[:, tokens], preferred_element_type=F32)
                scores[part, c] = block
                for lane in range(0, CHUNK, 128):
                    top = block[:, lane : lane + 128]
                    highest = top if highest is None else jnp.maximum(highest, top)
            if part > 0:
                weights = jnp.exp2(scores[part - 1, c] - offset).astype(BF16)
                product = lax.dot_general(weights, values[:, tokens], NT, preferred_element_type=F32)
                total = product if total is None else total + product
        if part > 0:
            result[part - 1] = total
        if part < 2:
            offset = jnp.max(highest, axis=1, keepdims=True)
    one = result[0, :, 0:width] / result[0, :, width : width + 1]
    two = result[1, :, 0:width] / result[1, :, width : width + 1]
    attended_ref[...] = jnp.where(first_head, one, two).T.astype(BF16)


def attention(micro, where, blocks, modulation, w_qkv, cache, earlier):
    width, model = w_qkv.shape[1], w_qkv.shape[2]
    extra = [earlier] if micro else []
    return pl.pallas_call(
        functools.partial(attention_kernel, micro, len(blocks)),
        out_shape=[
            jax.ShapeDtypeStruct((2, width, PATCH_TOK), BF16),
            jax.ShapeDtypeStruct((width, PATCH_TOK), BF16),
        ],
        in_specs=[SMEM] + [HBM] * len(blocks) + [VMEM] + [HBM] * 2 + [VMEM] * len(extra),
        out_specs=[VMEM] * 2,
        scratch_shapes=[
            pltpu.VMEM((PATCH_TOK, model), BF16),
            pltpu.VMEM(w_qkv.shape, BF16),
            pltpu.VMEM((width, PATCHES * PATCH_TOK), BF16),
            pltpu.VMEM((width + 16, PATCHES * PATCH_TOK), BF16),
            pltpu.VMEM((2 * PATCH_TOK, width), BF16),
            pltpu.VMEM((2, cache.shape[2] // CHUNK, PATCH_TOK, CHUNK), F32),
            pltpu.VMEM((2, PATCH_TOK, width + 16), F32),
            pltpu.SemaphoreType.DMA((4,)),
        ],
        compiler_params=pltpu.CompilerParams(vmem_limit_bytes=60 * 2**20),
        cost_estimate=pl.CostEstimate(
            flops=4 * 10**9, bytes_accessed=8 * 10**6, transcendentals=5 * 10**6
        ),
        name="attention",
    )(where, *blocks, modulation, w_qkv, cache, *extra)


def mlp_kernel(count, where_ref, *refs):
    blocks, refs = refs[:count], refs[count:]
    heads, refs = refs[:8], refs[8:]
    outs, refs = refs[:8], refs[8:]
    up_hbm, down_hbm, mod, *refs = refs
    parts, refs = refs[:COLUMNS], refs[COLUMNS:]
    inputs, attended, w_out, w_up, w_down, after, lowered, sem = refs
    column, row = where_ref[2], where_ref[3]
    width = heads[0].shape[0]
    out_copies = [
        pltpu.make_async_copy(
            from_all[n], whole.at[pl.ds(n * width, width)], sem.at[4 + n * 1 // 8]
        )
        for n in range(8)
        for whole, from_all in ((attended, heads), (w_out, outs))
    ]
    block_copies = patch_copies(blocks, inputs, column, row, sem.at[1])
    up_copy = pltpu.make_async_copy(up_hbm, w_up, sem.at[2])
    down_copy = pltpu.make_async_copy(down_hbm, w_down, sem.at[3])
    for copy in out_copies:
        copy.start()
    mixed = None
    per = 16 // 1
    for part in range(1):
        for copy in out_copies[part * per : (part + 1) * per]:
            copy.wait()
        if part == 0:
            for copy in block_copies + [up_copy, down_copy]:
                copy.start()
        feats = slice(part * per // 2 * width, (part + 1) * per // 2 * width)
        product = lax.dot_general(
            attended[feats, :], w_out[feats, :], TN, preferred_element_type=F32
        )
        mixed = product if mixed is None else mixed + product
    for copy in block_copies:
        copy.wait()
    after_attn = inputs[...].astype(F32) + mod[2:3, :] * mixed
    after[...] = after_attn
    mlp_in = (layer_norm(after_attn) * (1.0 + mod[4:5, :]) + mod[3:4, :]).astype(BF16)
    up_copy.wait()
    lifted = lax.dot_general(mlp_in, w_up[...], NT, preferred_element_type=F32)
    hidden = jax.nn.gelu(lifted, approximate=True).astype(BF16)
    down_copy.wait()
    lowered[...] = jnp.dot(hidden, w_down[...], preferred_element_type=F32) * mod[5:6, :]
    own = pl.ds(place(column, row, 0, HALF, 0), HALF)
    lowered[own, :] = lowered[own, :] + after[own, :]
    for k in range(COLUMNS):
        parts[k][...] = lowered[pl.ds(place(column, row, k, PAIR, 0), PAIR), :].astype(BF16)


def mlp(where, blocks, heads, outs, w_up, w_down, modulation):
    model = w_up.shape[1]
    return pl.pallas_call(
        functools.partial(mlp_kernel, len(blocks)),
        out_shape=[jax.ShapeDtypeStruct((PAIR, model), BF16)] * COLUMNS,
        in_specs=[SMEM] + [HBM] * (len(blocks) + 18) + [VMEM],
        out_specs=[VMEM] * COLUMNS,
        scratch_shapes=[
            pltpu.VMEM((PATCH_TOK, model), BF16),
            pltpu.VMEM((model, PATCH_TOK), BF16),
            pltpu.VMEM((model, model), BF16),
            pltpu.VMEM(w_up.shape, BF16),
            pltpu.VMEM(w_down.shape, BF16),
            pltpu.VMEM((PATCH_TOK, model), F32),
            pltpu.VMEM((PATCH_TOK, model), F32),
            pltpu.SemaphoreType.DMA((5,)),
        ],
        compiler_params=pltpu.CompilerParams(vmem_limit_bytes=60 * 2**20),
        cost_estimate=pl.CostEstimate(
            flops=2 * 10**9, bytes_accessed=8 * 10**6, transcendentals=2 * 10**5
        ),
        name="mlp",
    )(where, *blocks, *heads, *outs, w_up, w_down, modulation)


def summed(blocks):
    return sum(block.astype(F32) for block in blocks)


def gather_columns(block):
    return [block] + [to_column(block, -k) for k in range(1, COLUMNS)]


def gather_heads(block):
    own = gather_columns(block)
    return own + gather_columns(swap_rows(block))


def local(
    carry_x,
    kv_buffer,
    qkv_weight,
    out_weight,
    up_weight,
    down_weight,
    time_table,
    block_table,
    time_index,
    patch_order,
):
    section_index = lax.axis_index("section")
    head_index = lax.axis_index("head")
    column = head_index // 2
    row = head_index % 2
    chosen = jnp.arange(STEPS) == time_index[0]
    modulation = (
        jnp.sum(jnp.where(chosen[:, None, None], time_table, jnp.float32(0.0)), axis=0)
        + block_table[0]
    )
    patches = [patch_of(patch_order, section_index, m) for m in range(MICRO)]
    where = jnp.stack([*patches, column, row]).astype(jnp.int32)
    inputs, w_out = carry_x[0], out_weight[0]
    own_outs = [w_out, to_column(w_out, -1), None, to_column(w_out, -3)]
    own_blocks, partner, w_out = lax.optimization_barrier(
        (gather_columns(inputs), swap_rows(inputs), w_out)
    )
    blocks, own_outs, w_out, partner_out = lax.optimization_barrier(
        (own_blocks + gather_columns(partner), own_outs, w_out, swap_rows(w_out))
    )
    own_outs[2] = to_column(w_out, -2)
    outs = own_outs + gather_columns(partner_out)
    fresh_list = []
    for micro in range(MICRO):
        fresh, attended = attention(
            micro,
            where,
            blocks,
            modulation,
            qkv_weight[0],
            kv_buffer[0],
            fresh_list[0] if micro else None,
        )
        fresh_list.append(fresh)
        if micro == 0:
            attended, outs = lax.optimization_barrier((attended, outs))
        parts = mlp(
            where,
            blocks,
            gather_heads(attended),
            outs,
            up_weight[0].T,
            down_weight[0].T,
            modulation,
        )
        row_sum = summed([to_section(parts[k], k) for k in range(COLUMNS)])
        if micro + 1 < MICRO:
            row_sum = row_sum.astype(BF16)
            both = row_sum.astype(F32) + swap_rows(row_sum).astype(F32)
            blocks = gather_columns(both.astype(BF16))
        else:
            mine = jnp.where(row == 0, row_sum[:HALF], row_sum[HALF:])
            theirs = jnp.where(row == 0, row_sum[HALF:], row_sum[:HALF]).astype(BF16)
            outgoing = (mine + swap_rows(theirs).astype(F32)).astype(BF16)
    return (outgoing[None], jnp.stack(fresh_list)[None])


def solution(mesh):
    placed = (
        P("section", "head", None),
        P("section", None, "head", None),
        P("section", None, "head", None),
        P("section", "head", None),
        P("section", None, "head"),
        P("section", None, "head"),
        P(),
        P("section", None, None),
        P("section"),
        P(),
    )
    return jax.shard_map(
        local,
        mesh=mesh,
        in_specs=placed,
        out_specs=(P("section", "head", None), P("section", None, None, "head", None)),
        check_vma=False,
    )
```
